32 devices in a mesh: groups: 2 (over x), expert: 8 (over z, y), tensor: 2 (over core).
Axes of the slice: x: 2, y: 2, z: 4, core: 2. Of those that a mesh axis runs over, the one named last changes fastest.
Arguments:
- quant_rows: bfloat16 [512, 3072], P(('groups', 'expert', 'tensor')), parts along dimension 0, may hold values from -6 to 6
- block_exps: int32 [512, 24], P(('groups', 'expert', 'tensor')), parts along dimension 0, may hold values from -2 to 1
- expert_ids: int32 [512, 4], P(('groups', 'expert', 'tensor')), parts along dimension 0, may hold values from 0 to 7, all different within a row; in each aligned block of 16 rows (0 to 15, 16 to 31, ...) at most 8 rows name the same one
- route_weights: float32 [512, 4], P(('groups', 'expert', 'tensor')), parts along dimension 0, may hold values from 0.1 to 1
- gate_weight: bfloat16 [8, 3072, 5376], P('expert', None, 'tensor'), may hold values from -0.109375 to 0.109375
- up_weight: bfloat16 [8, 3072, 5376], P('expert', None, 'tensor'), may hold values from -0.109375 to 0.109375
- down_weight: bfloat16 [8, 5376, 3072], P('expert', 'tensor'), may hold values from -0.078125 to 0.078125
- cotangent: bfloat16 [512, 3072], P(('groups', 'expert', 'tensor')), parts along dimension 0, may hold values from -6 to 6
Outputs:
- mixed: bfloat16 [512, 3072], P(('groups', 'expert', 'tensor')), parts along dimension 0
- grad_tokens: bfloat16 [512, 3072], P(('groups', 'expert', 'tensor')), parts along dimension 0
- grad_weights: float32 [512, 4], P(('groups', 'expert', 'tensor')), parts along dimension 0
The draws below stay inside these ranges and needn't reach their ends.
There are 2 independent parts, one for each index of `groups`. The reference program is written for one: setup_inputs(seed, part) draws one part's arguments, and reference() takes and returns one part's arrays. A program takes and returns all parts, laid end to end along the dimension named above; an argument that names none is the same for every part. Nothing has to cross between parts.
Inputs may be any that keep to these rules, and one draw needn't show every extreme that they name: `expert_ids`: each token names 4 different experts. In each aligned block of 16 tokens (the tokens of one device) no expert is named by more than 8 tokens, a bound that some block reaches.
All inputs are finite; a program needn't handle non-finite values.
Results may differ from the reference program's by a relative error of at most 0.0064.
Values may be sent and summed in bfloat16 or wider, within the bound.
A program may use at most 128 MiB of HBM per device.

```python
import math
import jax
import jax.numpy as jnp
import numpy as np
from jax import lax

D = 3072
FF = 5376
BLOCK = 128
TOPK = 4
TOK_DEV = 16
CAP = 8
EXPERTS = 8
TOKENS = 256
N_EXPERT = 8
N_TENSOR = 2


def plant(result, key, least, top_value):
    longest = result.shape.index(max(result.shape))
    spots = []
    for shift in (0, 1):
        where = [jax.random.randint(jax.random.fold_in(key, axis), (), 0, length) for axis, length in enumerate(result.shape)]
        where[longest] = (where[longest] + shift) % result.shape[longest]
        spots.append(tuple(where))
    return result.at[spots[0]].set(least).at[spots[1]].set(top_value)


def level_of(key, shape, cuts, smallest, high):
    def one(axis_at, parts):
        steps = jax.random.uniform(jax.random.fold_in(jax.random.fold_in(key, 6), axis_at), (parts,), jnp.float32, smallest / len(cuts), high / len(cuts))
        return jnp.repeat(jnp.exp(steps), shape[axis_at] // parts).reshape((-1,) + (1,) * (len(shape) - axis_at - 1))

    loudness = one(*cuts[0])
    for cut in cuts[1:]:
        loudness = loudness * one(*cut)
    return loudness


def deal_out(own_key, own, number, rows, count, top, most, lean):
    order = jax.random.permutation(own_key, count)
    packed, usual = portions_of(count, rows * top, most, lean, True), portions_of(count, rows * top, most, lean, False)
    places = jnp.arange(count)

    def named(tallies, offset_by):
        used = int((tallies > 0).sum())
        fixed = max(1, used // 4)
        shifted = fixed + (places - fixed + offset_by * (used - fixed)) % max(1, count - fixed)
        return jnp.zeros((count,), jnp.int32).at[order[jnp.where(places < fixed, places, shifted)]].set(jnp.asarray(tallies, jnp.int32))

    tallies = jnp.where(number % 4 == 0, named(packed, number // 4), named(usual, number - number // 4 - 1))
    mixed = jax.random.permutation(jax.random.fold_in(own, 3), count)
    giver, taker = mixed[0:count // 2 * 2:2], mixed[1:count // 2 * 2:2]
    margin = jnp.minimum(tallies[giver] - 1, most - tallies[taker]) // 2
    margin = jnp.where((giver == order[0]) | (taker == order[0]) | (tallies[taker] == 0), 0, jnp.maximum(margin, 0))
    shifted = jax.random.randint(jax.random.fold_in(own, 4), (count // 2,), 0, 1 << 20) % (margin + 1)
    tallies = tallies.at[giver].add(-shifted).at[taker].add(shifted)
    members = jnp.searchsorted(jnp.cumsum(tallies), jnp.arange(rows * top), side="right").astype(jnp.int32)
    grid = members.reshape(top, rows).T
    grid = grid[jax.random.permutation(jax.random.fold_in(own, 1), rows)]
    offset_by = jax.random.randint(jax.random.fold_in(own, 2), (rows, 1), 0, top)
    return jnp.take_along_axis(grid, (jnp.arange(top)[None, :] + offset_by) % top, axis=1)


def portions_of(count, total, most, slope, full):
    weights = [(1 << 20) // math.isqrt(standing ** slope) + 1 for standing in range(1, count + 1)]
    largest = most if full else min(most, max(-(-total // count), total * weights[0] // sum(weights)))
    least = 1 if total - largest >= count - 1 else 0
    counts, surplus = [largest] + [least] * (count - 1), total - largest - least * (count - 1)
    while surplus > 0:
        candidates = [i for i in range(1, count) if counts[i] < largest] or [i for i in range(1, count) if counts[i] < most]
        mass, remaining = sum([weights[i] for i in candidates]), surplus
        for i in candidates:
            addition = min(most - counts[i], max(1, remaining * weights[i] // mass), surplus)
            counts[i] = counts[i] + addition
            surplus = surplus - addition
    return np.array(counts)


def centred(own_key, dims, spread, most, cuts=(), held_as=jnp.bfloat16):
    array = spread * jax.random.normal(own_key, dims, jnp.float32)
    if cuts:
        array = array * level_of(own_key, dims, cuts, -0.22, 0.18)
    return jnp.clip(array, -most, most).astype(held_as)


def setup_inputs(seed: int = 0, part: int = 0) -> dict:
    seeds = jax.random.split(jax.random.key(seed), 9)
    part_keys = jax.random.split(jax.random.fold_in(seeds[8], part), 9)
    quant_rows = centred(part_keys[0], (TOKENS, D), 1.0, 6.0, ((0, 16),))
    block_exps = plant(jax.random.randint(part_keys[1], (TOKENS, D // BLOCK), -2, 2), jax.random.fold_in(part_keys[1], 1), -2, 1).astype(jnp.int32)
    expert_ids_keys = jax.random.split(jax.random.fold_in(part_keys[2], 1), TOKENS // TOK_DEV)
    expert_ids_turns = jax.random.permutation(jax.random.fold_in(part_keys[2], 3), TOKENS // TOK_DEV)
    expert_ids = jax.vmap(lambda own, number: deal_out(jax.random.fold_in(part_keys[2], 2), own, number, TOK_DEV, EXPERTS, TOPK, CAP, 2))(expert_ids_keys, expert_ids_turns).reshape((TOKENS, TOPK))
    route_weights = jnp.clip(jnp.exp(math.log(1.0) - 2.3025851 * jax.random.uniform(part_keys[3], (TOKENS, TOPK), jnp.float32) ** level_of(part_keys[3], (TOKENS, TOPK), ((0, 16),), -0.2, 0.2)), 0.1, 1.0)
    gate_weight = centred(seeds[4], (EXPERTS, D, FF), D ** -0.5, 0.109375, ((0, 8), (2, 2)))
    up_weight = centred(seeds[5], (EXPERTS, D, FF), D ** -0.5, 0.109375, ((0, 8), (2, 2)))
    down_weight = centred(seeds[6], (EXPERTS, FF, D), FF ** -0.5, 0.078125, ((0, 8), (1, 2)))
    cotangent = centred(part_keys[7], (TOKENS, D), 1.0, 6.0, ((0, 16),))
    return dict(quant_rows=quant_rows, block_exps=block_exps, expert_ids=expert_ids, route_weights=route_weights, gate_weight=gate_weight, up_weight=up_weight, down_weight=down_weight, cotangent=cotangent)


def expert_pass(rows, grads, gate_w, up_w, down_w):
    gate = jnp.dot(rows, gate_w, preferred_element_type=jnp.float32)
    up = jnp.dot(rows, up_w, preferred_element_type=jnp.float32)
    sig = jax.nn.sigmoid(gate)
    act = gate * sig
    hidden = (act * up).astype(jnp.bfloat16)
    out_part = jnp.dot(hidden, down_w, preferred_element_type=jnp.float32)
    back = jnp.dot(grads, down_w.T, preferred_element_type=jnp.float32)
    d_gate = (back * up * sig * (1.0 + gate * (1.0 - sig))).astype(jnp.bfloat16)
    d_up = (back * act).astype(jnp.bfloat16)
    in_part = jnp.dot(d_gate, gate_w.T, preferred_element_type=jnp.float32)
    in_part = in_part + jnp.dot(d_up, up_w.T, preferred_element_type=jnp.float32)
    return out_part, in_part


def reference(quant_rows, block_exps, expert_ids, route_weights, gate_weight, up_weight, down_weight, cotangent):
    scales = jnp.exp2(block_exps.astype(jnp.float32))
    tokens = (quant_rows.astype(jnp.float32).reshape(TOKENS, D // BLOCK, BLOCK) * scales[:, :, None]).reshape(TOKENS, D).astype(jnp.bfloat16)
    limit = min(TOKENS, N_EXPERT * N_TENSOR * CAP)
    grad32 = cotangent.astype(jnp.float32)

    def step(carry, expert):
        out_acc, gx_acc, gw_acc = carry
        hits = expert_ids == expert
        mask = jnp.any(hits, axis=1)
        weight = jnp.sum(jnp.where(hits, route_weights, jnp.float32(0.0)), axis=1)
        order = jnp.argsort((1 - mask.astype(jnp.int32)).astype(jnp.int32), stable=True)[:limit].astype(jnp.int32)
        valid = mask[order]
        rows = jnp.where(valid[:, None], tokens[order], jnp.zeros((), jnp.bfloat16))
        grads = (weight[order][:, None] * grad32[order]).astype(jnp.bfloat16)
        out_part, in_part = expert_pass(rows, grads, gate_weight[expert], up_weight[expert], down_weight[expert])
        y_low = lax.optimization_barrier(out_part.astype(jnp.bfloat16))
        dx_low = lax.optimization_barrier(in_part.astype(jnp.bfloat16))
        y_val = y_low.astype(jnp.float32)
        dx_val = dx_low.astype(jnp.float32)
        keep = valid.astype(jnp.float32)[:, None]
        out_acc = out_acc.at[order].add(weight[order][:, None] * y_val * keep)
        gx_acc = gx_acc.at[order].add(dx_val * keep)
        dots = jnp.sum(grad32[order] * y_val, axis=1) * valid.astype(jnp.float32)
        gw_acc = gw_acc.at[order].add(dots[:, None] * hits[order].astype(jnp.float32))
        return (out_acc, gx_acc, gw_acc), None

    start = (jnp.zeros((TOKENS, D), jnp.float32), jnp.zeros((TOKENS, D), jnp.float32), jnp.zeros((TOKENS, TOPK), jnp.float32))
    (out_acc, gx_acc, gw_acc), _ = lax.scan(step, start, jnp.arange(EXPERTS, dtype=jnp.int32))
    return out_acc.astype(jnp.bfloat16), gx_acc.astype(jnp.bfloat16), gw_acc
```

```python
import functools

import jax
import jax.numpy as jnp
from jax import lax
from jax.experimental import pallas as pl
from jax.experimental.pallas import tpu as pltpu
from jax.sharding import PartitionSpec as P

CAP = 8

MESH = pl.DeviceIdType.MESH
NT = (((1,), (1,)), ((), ()))
CHUNKS = 4
F_TILES = 3
D_TILES = 3
E_TILES = 7


def fused_kernel(
    experts,
    xg_hbm,
    gate_hbm,
    up_hbm,
    down_hbm,
    ret_hbm,
    gw,
    uw,
    dw,
    rx,
    acc,
    hid,
    own,
    pair_out,
    pair_in,
    back_out,
    w_sem,
    d_send,
    d_recv,
    f_send,
    f_recv,
    p_send,
    p_recv,
    r_send,
    r_recv,
):
    chunks, dc, ff = gw.shape
    half = experts * CAP
    me = lax.axis_index("expert")
    core = lax.axis_index("tensor")
    mate = {"tensor": 1 - core}

    def weight_copies(c):
        cols = pl.ds(c * dc, dc)
        return (
            pltpu.make_async_copy(gate_hbm.at[cols, :], gw.at[c], w_sem.at[0, c]),
            pltpu.make_async_copy(up_hbm.at[cols, :], uw.at[c], w_sem.at[1, c]),
            pltpu.make_async_copy(down_hbm.at[:, cols], dw.at[c], w_sem.at[2, c]),
        )

    def own_copy(c):
        return pltpu.make_async_copy(
            xg_hbm.at[me, :, pl.ds(c * dc, dc)], rx.at[c, 0, 0], d_recv.at[c, 0]
        )

    def dispatch(c, j):
        peer = lax.rem(me + j, experts)
        return pltpu.make_async_remote_copy(
            src_ref=xg_hbm.at[peer, :, pl.ds(c * dc, dc)],
            dst_ref=rx.at[c, 0, j],
            send_sem=d_send.at[c, j],
            recv_sem=d_recv.at[c, j],
            device_id={"expert": peer},
            device_id_type=MESH,
        )

    def forward(c):
        return pltpu.make_async_remote_copy(
            src_ref=rx.at[c, 0],
            dst_ref=rx.at[c, 1],
            send_sem=f_send.at[c],
            recv_sem=f_recv.at[c],
            device_id=mate,
            device_id_type=MESH,
        )

    def pair(c):
        return pltpu.make_async_remote_copy(
            src_ref=pair_out.at[c % 2],
            dst_ref=pair_in.at[c],
            send_sem=p_send.at[c],
            recv_sem=p_recv.at[c],
            device_id=mate,
            device_id_type=MESH,
        )

    def own_back(c):
        return pltpu.make_async_copy(
            back_out.at[c, 0], ret_hbm.at[me, :, pl.ds(c * dc, dc)], r_recv.at[c, 0]
        )

    def give_back(c, j):
        return pltpu.make_async_remote_copy(
            src_ref=back_out.at[c, j],
            dst_ref=ret_hbm.at[me, :, pl.ds(c * dc, dc)],
            send_sem=r_send.at[c, j],
            recv_sem=r_recv.at[c, j],
            device_id={"expert": lax.rem(me + experts - j, experts)},
            device_id_type=MESH,
        )

    for copy in weight_copies(0):
        copy.start()

    barrier = pltpu.get_barrier_semaphore()
    for j in range(1, experts):
        pl.semaphore_signal(
            barrier,
            inc=1,
            device_id={"expert": lax.rem(me + j, experts)},
            device_id_type=MESH,
        )
    pl.semaphore_signal(barrier, inc=1, device_id=mate, device_id_type=MESH)
    pl.semaphore_wait(barrier, experts)

    for c in range(chunks):
        own_copy(c).start()
        for j in range(1, experts):
            dispatch(c, j).start()
    for c in range(1, chunks):
        for copy in weight_copies(c):
            copy.start()

    def collect(c):
        own_copy(c).wait()
        for j in range(1, experts):
            dispatch(c, j).wait_recv()
        forward(c).start()

    f_tile = ff // F_TILES
    collect(0)
    for c in range(chunks):
        if c + 1 < chunks:
            collect(c + 1)
        forward(c).wait_recv()
        for copy in weight_copies(c):
            copy.wait()
        both = rx[c].astype(jnp.float32)
        xs = both[:, :, :CAP, :].reshape(2 * half, dc).astype(jnp.bfloat16)
        gs = both[:, :, CAP:, :].reshape(2 * half, dc).astype(jnp.bfloat16)
        for f in range(F_TILES):
            cols = pl.ds(f * f_tile, f_tile)
            gate = jnp.dot(xs, gw[c, :, cols], preferred_element_type=jnp.float32)
            up = jnp.dot(xs, uw[c, :, cols], preferred_element_type=jnp.float32)
            back = lax.dot_general(gs, dw[c, cols, :], NT, preferred_element_type=jnp.float32)
            if c == 0:
                acc[0, :, cols] = gate
                acc[1, :, cols] = up
                acc[2, :, cols] = back
            else:
                acc[0, :, cols] += gate
                acc[1, :, cols] += up
                acc[2, :, cols] += back

    e_tile = ff // E_TILES
    for e in range(E_TILES):
        cols = pl.ds(e * e_tile, e_tile)
        gate = acc[0, :, cols]
        up = acc[1, :, cols]
        back = acc[2, :, cols]
        sig = jax.nn.sigmoid(gate)
        act = gate * sig
        hid[0, :, cols] = (act * up).astype(jnp.bfloat16)
        hid[1, :, cols] = (back * up * sig * (1.0 + gate * (1.0 - sig))).astype(jnp.bfloat16)
        hid[2, :, cols] = (back * act).astype(jnp.bfloat16)

    def finish(c):
        pair(c).wait_recv()
        tot = own[c % 2] + pair_in[c]
        back_out[c] = tot.astype(jnp.bfloat16)
        for j in range(1, experts):
            give_back(c, j).start()
        own_back(c).start()

    d_tile = dc // D_TILES
    for c in range(chunks):
        if c >= 2:
            pair(c - 2).wait_send()
        for d in range(D_TILES):
            cols = pl.ds(d * d_tile, d_tile)
            y = jnp.dot(hid[0], dw[c, :, cols], preferred_element_type=jnp.float32)
            dx = lax.dot_general(hid[1], gw[c, cols, :], NT, preferred_element_type=jnp.float32)
            dx = dx + lax.dot_general(
                hid[2], uw[c, cols, :], NT, preferred_element_type=jnp.float32
            )
            y = y.reshape(2, experts, CAP, d_tile)
            dx = dx.reshape(2, experts, CAP, d_tile)
            own[c % 2, :, :CAP, cols] = y[0]
            own[c % 2, :, CAP:, cols] = dx[0]
            pair_out[c % 2, :, :CAP, cols] = y[1]
            pair_out[c % 2, :, CAP:, cols] = dx[1]
        pair(c).start()
        if c >= 1:
            finish(c - 1)
    finish(chunks - 1)

    for c in range(chunks):
        forward(c).wait_send()
        if c >= chunks - 2:
            pair(c).wait_send()
        own_back(c).wait()
        for j in range(1, experts):
            dispatch(c, j).wait_send()
            give_back(c, j).wait_send()
            give_back(c, j).wait_recv()


def fused_experts(xg, gate_w, up_w, down_w):
    experts, _, width = xg.shape
    ff = gate_w.shape[1]
    c, dc, rows = CHUNKS, width // CHUNKS, 2 * experts * CAP
    dma = pltpu.SemaphoreType.DMA
    return pl.pallas_call(
        functools.partial(fused_kernel, experts),
        out_shape=jax.ShapeDtypeStruct(xg.shape, jnp.bfloat16),
        in_specs=[pl.BlockSpec(memory_space=pl.ANY)] * 4,
        out_specs=pl.BlockSpec(memory_space=pl.ANY),
        scratch_shapes=[
            pltpu.VMEM((c, dc, ff), jnp.bfloat16),
            pltpu.VMEM((c, dc, ff), jnp.bfloat16),
            pltpu.VMEM((c, ff, dc), jnp.bfloat16),
            pltpu.VMEM((c, 2, experts, 2 * CAP, dc), jnp.bfloat16),
            pltpu.VMEM((3, rows, ff), jnp.float32),
            pltpu.VMEM((3, rows, ff), jnp.bfloat16),
            pltpu.VMEM((2, experts, 2 * CAP, dc), jnp.float32),
            pltpu.VMEM((2, experts, 2 * CAP, dc), jnp.float32),
            pltpu.VMEM((c, experts, 2 * CAP, dc), jnp.float32),
            pltpu.VMEM((c, experts, 2 * CAP, dc), jnp.bfloat16),
            dma((3, c)),
            dma((c, experts)),
            dma((c, experts)),
            dma((c,)),
            dma((c,)),
            dma((c,)),
            dma((c,)),
            dma((c, experts)),
            dma((c, experts)),
        ],
        compiler_params=pltpu.CompilerParams(
            collective_id=0, has_side_effects=True, vmem_limit_bytes=63 * 2**20
        ),
        cost_estimate=pl.CostEstimate(
            flops=12 * rows * width * ff, bytes_accessed=6 * width * ff, transcendentals=rows * ff
        ),
    )(xg, gate_w, up_w, down_w)


def expert_pass(rows, grads, gate_w, up_w, down_w):
    gate = jnp.dot(rows, gate_w, preferred_element_type=jnp.float32)
    up = jnp.dot(rows, up_w, preferred_element_type=jnp.float32)
    sig = jax.nn.sigmoid(gate)
    act = gate * sig
    hidden = (act * up).astype(jnp.bfloat16)
    out_part = jnp.dot(hidden, down_w, preferred_element_type=jnp.float32)
    back = lax.dot_general(
        grads, down_w, (((1,), (1,)), ((), ())), preferred_element_type=jnp.float32
    )
    d_gate = (back * up * sig * (1.0 + gate * (1.0 - sig))).astype(jnp.bfloat16)
    d_up = (back * act).astype(jnp.bfloat16)
    in_part = lax.dot_general(
        d_gate, gate_w, (((1,), (1,)), ((), ())), preferred_element_type=jnp.float32
    )
    in_part = in_part + lax.dot_general(
        d_up, up_w, (((1,), (1,)), ((), ())), preferred_element_type=jnp.float32
    )
    return (out_part, in_part)


def exchange(send_x, send_g, gate_w, up_w, down_w, experts, pair, width):
    dup_x = jnp.broadcast_to(send_x[:, None], (experts, pair, CAP, width)).reshape(
        experts * pair, CAP, width
    )
    dup_g = jnp.broadcast_to(send_g[:, None], (experts, pair, CAP, width)).reshape(
        experts * pair, CAP, width
    )
    got_x, got_g = (
        lax.all_to_all(dup_x, ("expert", "tensor"), split_axis=0, concat_axis=0, tiled=True),
        lax.all_to_all(dup_g, ("expert", "tensor"), split_axis=0, concat_axis=0, tiled=True),
    )
    out_part, in_part = expert_pass(
        got_x.reshape(-1, width), got_g.reshape(-1, width), gate_w, up_w, down_w
    )
    back_y, back_dx = (
        lax.all_to_all(
            out_part.reshape(experts * pair, CAP, width),
            ("expert", "tensor"),
            split_axis=0,
            concat_axis=0,
            tiled=True,
        ),
        lax.all_to_all(
            in_part.reshape(experts * pair, CAP, width),
            ("expert", "tensor"),
            split_axis=0,
            concat_axis=0,
            tiled=True,
        ),
    )
    y_back = (
        jnp.sum(back_y.reshape(experts, pair, CAP, width), axis=1)
        .astype(jnp.bfloat16)
        .reshape(experts * CAP, width)
    )
    dx_back = (
        jnp.sum(back_dx.reshape(experts, pair, CAP, width), axis=1)
        .astype(jnp.bfloat16)
        .reshape(experts * CAP, width)
    )
    return (y_back, dx_back)


def body(
    quant_rows,
    block_exps,
    expert_ids,
    route_weights,
    gate_weight,
    up_weight,
    down_weight,
    cotangent,
):
    tok_rows, width = quant_rows.shape
    blocks = block_exps.shape[1]
    picks = expert_ids.shape[1]
    experts = lax.axis_size("expert")
    pair = lax.axis_size("tensor")
    scales = jnp.exp2(block_exps.astype(jnp.float32))
    tokens = (
        (
            quant_rows.astype(jnp.float32).reshape(tok_rows, blocks, width // blocks)
            * scales[:, :, None]
        )
        .reshape(tok_rows, width)
        .astype(jnp.bfloat16)
    )
    flat_ids = expert_ids.reshape(-1)
    onehot = (flat_ids[:, None] == jnp.arange(experts, dtype=jnp.int32)[None, :]).astype(jnp.int32)
    before = jnp.cumsum(onehot, axis=0) - onehot
    slot = jnp.sum(before * onehot, axis=1)
    target = flat_ids * CAP + slot
    placer = (jnp.arange(experts * CAP, dtype=jnp.int32)[:, None] == target[None, :]).astype(
        jnp.bfloat16
    )
    placer_tok = jnp.sum(
        placer.reshape(experts * CAP, tok_rows, picks).astype(jnp.float32), axis=2
    ).astype(jnp.bfloat16)
    grad32 = cotangent.astype(jnp.float32)
    scaled_grad = (
        (route_weights[:, :, None] * grad32[:, None, :])
        .astype(jnp.bfloat16)
        .reshape(tok_rows * picks, width)
    )
    send_x = (
        jnp.dot(placer_tok, tokens, preferred_element_type=jnp.float32)
        .astype(jnp.bfloat16)
        .reshape(experts, CAP, width)
    )
    send_g = (
        jnp.dot(placer, scaled_grad, preferred_element_type=jnp.float32)
        .astype(jnp.bfloat16)
        .reshape(experts, CAP, width)
    )
    gate_w = gate_weight[0]
    up_w = up_weight[0]
    down_w = down_weight[0]
    if experts <= 8:
        ret = fused_experts(jnp.concatenate([send_x, send_g], axis=1), gate_w, up_w, down_w)
        y_back = ret[:, :CAP].reshape(experts * CAP, width)
        dx_back = ret[:, CAP:].reshape(experts * CAP, width)
    else:
        y_back, dx_back = exchange(send_x, send_g, gate_w, up_w, down_w, experts, pair, width)
    picked_y = lax.dot_general(
        placer, y_back, (((0,), (0,)), ((), ())), preferred_element_type=jnp.float32
    ).reshape(tok_rows, picks, width)
    picked_dx = lax.dot_general(
        placer, dx_back, (((0,), (0,)), ((), ())), preferred_element_type=jnp.float32
    ).reshape(tok_rows, picks, width)
    mixed = jnp.sum(route_weights[:, :, None] * picked_y, axis=1).astype(jnp.bfloat16)
    grad_tokens = jnp.sum(picked_dx, axis=1).astype(jnp.bfloat16)
    grad_weights = jnp.sum(grad32[:, None, :] * picked_y, axis=2)
    return (mixed, grad_tokens, grad_weights)


def solution(mesh):
    in_specs = (
        P(("groups", "expert", "tensor"), None),
        P(("groups", "expert", "tensor"), None),
        P(("groups", "expert", "tensor"), None),
        P(("groups", "expert", "tensor"), None),
        P("expert", None, "tensor"),
        P("expert", None, "tensor"),
        P("expert", "tensor", None),
        P(("groups", "expert", "tensor"), None),
    )
    out_specs = (
        P(("groups", "expert", "tensor"), None),
        P(("groups", "expert", "tensor"), None),
        P(("groups", "expert", "tensor"), None),
    )
    return jax.shard_map(body, mesh=mesh, in_specs=in_specs, out_specs=out_specs, check_vma=False)
```

```python
import functools

import jax
import jax.numpy as jnp
from jax import lax
from jax.experimental import pallas as pl
from jax.experimental.pallas import tpu as pltpu
from jax.sharding import PartitionSpec as P

CAP = 8

MESH = pl.DeviceIdType.MESH
NT = (((1,), (1,)), ((), ()))
TN = (((0,), (0,)), ((), ()))
BLOCK = 128
CHUNKS = 6
F_TILES = 3
D_TILES = 2
E_TILES = 7


def fused_kernel(
    experts,
    q_ref,
    exp_ref,
    ids_ref,
    wts_ref,
    cot_ref,
    gate_hbm,
    up_hbm,
    down_hbm,
    mixed_ref,
    gtok_ref,
    gwts_ref,
    xg,
    ret,
    gw,
    uw,
    dw,
    rx,
    acc,
    hid,
    own,
    pair_out,
    pair_in,
    w_sem,
    d_send,
    d_recv,
    f_send,
    f_recv,
    p_send,
    p_recv,
    r_send,
    r_recv,
):
    chunks, dc, ff = gw.shape
    half = experts * CAP
    me = lax.axis_index("expert")
    core = lax.axis_index("tensor")
    mate = {"tensor": 1 - core}

    def weight_copies(c):
        cols = pl.ds(pl.multiple_of(c * dc, dc), dc)
        return (
            pltpu.make_async_copy(gate_hbm.at[cols, :], gw.at[c], w_sem.at[0, c]),
            pltpu.make_async_copy(up_hbm.at[cols, :], uw.at[c], w_sem.at[1, c]),
            pltpu.make_async_copy(down_hbm.at[:, cols], dw.at[c], w_sem.at[2, c]),
        )

    def own_copy(c):
        return pltpu.make_async_copy(
            xg.at[c, me], rx.at[c, 0, 0], d_recv.at[c, 0]
        )

    def dispatch(c, j):
        peer = lax.rem(me + j, experts)
        return pltpu.make_async_remote_copy(
            src_ref=xg.at[c, peer],
            dst_ref=rx.at[c, 0, j],
            send_sem=d_send.at[c, j],
            recv_sem=d_recv.at[c, j],
            device_id={"expert": peer},
            device_id_type=MESH,
        )

    def forward(c):
        return pltpu.make_async_remote_copy(
            src_ref=rx.at[c, 0],
            dst_ref=rx.at[c, 1],
            send_sem=f_send.at[c],
            recv_sem=f_recv.at[c],
            device_id=mate,
            device_id_type=MESH,
        )

    def pair(c):
        return pltpu.make_async_remote_copy(
            src_ref=pair_out.at[c % 2],
            dst_ref=pair_in.at[c],
            send_sem=p_send.at[c],
            recv_sem=p_recv.at[c],
            device_id=mate,
            device_id_type=MESH,
        )

    def own_back(c):
        return pltpu.make_async_copy(
            xg.at[c, 0], ret.at[c, me], r_recv.at[c, 0]
        )

    def give_back(c, j):
        return pltpu.make_async_remote_copy(
            src_ref=xg.at[c, j],
            dst_ref=ret.at[c, me],
            send_sem=r_send.at[c, j],
            recv_sem=r_recv.at[c, j],
            device_id={"expert": lax.rem(me + experts - j, experts)},
            device_id_type=MESH,
        )

    for c in range(chunks):
        for copy in weight_copies(c):
            copy.start()

    toks, picks = ids_ref.shape
    ids = ids_ref[...]
    wts = wts_ref[...]
    place = lax.broadcasted_iota(jnp.int32, (toks, half), 1)
    hits = [(ids[:, k : k + 1] == place // CAP).astype(jnp.float32) for k in range(picks)]
    named = hits[0]
    for k in range(1, picks):
        named = named + hits[k]
    later = lax.broadcasted_iota(jnp.int32, (toks, toks), 0)
    earlier = lax.broadcasted_iota(jnp.int32, (toks, toks), 1)
    below = (earlier < later).astype(jnp.bfloat16)
    before = jnp.dot(below, named.astype(jnp.bfloat16), preferred_element_type=jnp.float32)
    in_slot = (before == (place % CAP).astype(jnp.float32)).astype(jnp.float32)
    placer = jnp.concatenate([hit * in_slot for hit in hits], axis=0).astype(jnp.bfloat16)
    placer_tok = (named * in_slot).astype(jnp.bfloat16)
    exps = exp_ref[...]
    scales = jnp.where(
        exps >= 0, jnp.where(exps == 1, 2.0, 1.0), jnp.where(exps == -1, 0.5, 0.25)
    ).astype(jnp.float32)

    def prepare(c):
        parts = []
        for b in range(c * dc // BLOCK, (c + 1) * dc // BLOCK):
            part = q_ref[:, b * BLOCK : (b + 1) * BLOCK].astype(jnp.float32)
            parts.append((part * scales[:, b : b + 1]).astype(jnp.bfloat16))
        toks_c = jnp.concatenate(parts, axis=1)
        grad32 = cot_ref[:, pl.ds(c * dc, dc)].astype(jnp.float32)
        scaled = jnp.concatenate([wts[:, k : k + 1] * grad32 for k in range(picks)], axis=0)
        xs = lax.dot_general(placer_tok, toks_c, TN, preferred_element_type=jnp.float32)
        gs = lax.dot_general(
            placer, scaled.astype(jnp.bfloat16), TN, preferred_element_type=jnp.float32
        )
        both = [xs.reshape(experts, CAP, dc), gs.reshape(experts, CAP, dc)]
        xg[c] = jnp.concatenate(both, axis=1).astype(jnp.bfloat16)

    prepare(0)
    barrier = pltpu.get_barrier_semaphore()
    for j in range(1, experts):
        pl.semaphore_signal(
            barrier,
            inc=1,
            device_id={"expert": lax.rem(me + j, experts)},
            device_id_type=MESH,
        )
    pl.semaphore_signal(barrier, inc=1, device_id=mate, device_id_type=MESH)
    pl.semaphore_wait(barrier, experts)

    for c in range(chunks):
        if c > 0:
            prepare(c)
        own_copy(c).start()
        for j in range(1, experts):
            dispatch(c, j).start()
    def collect(c):
        own_copy(c).wait()
        for j in range(1, experts):
            dispatch(c, j).wait_recv()
        forward(c).start()

    f_tile = ff // F_TILES
    def project(c):
        forward(c).wait_recv()
        for copy in weight_copies(c):
            copy.wait()
        both = rx[c].astype(jnp.float32)
        xs = both[:, :, :CAP, :].reshape(2 * half, dc).astype(jnp.bfloat16)
        gs = both[:, :, CAP:, :].reshape(2 * half, dc).astype(jnp.bfloat16)
        for f in range(F_TILES):
            cols = pl.ds(f * f_tile, f_tile)
            gate = jnp.dot(xs, gw[c, :, cols], preferred_element_type=jnp.float32)
            up = jnp.dot(xs, uw[c, :, cols], preferred_element_type=jnp.float32)
            back = lax.dot_general(gs, dw[c, cols, :], NT, preferred_element_type=jnp.float32)
            acc[0, :, cols] += gate
            acc[1, :, cols] += up
            acc[2, :, cols] += back

    acc[...] = jnp.zeros_like(acc)
    collect(0)

    @pl.loop(0, chunks)
    def _(c):
        @pl.when(c + 1 < chunks)
        def _():
            collect(c + 1)

        project(c)

    e_tile = ff // E_TILES
    for e in range(E_TILES):
        cols = pl.ds(e * e_tile, e_tile)
        gate = acc[0, :, cols]
        up = acc[1, :, cols]
        back = acc[2, :, cols]
        sig = jax.nn.sigmoid(gate)
        act = gate * sig
        hid[0, :, cols] = (act * up).astype(jnp.bfloat16)
        hid[1, :, cols] = (back * up * sig * (1.0 + gate * (1.0 - sig))).astype(jnp.bfloat16)
        hid[2, :, cols] = (back * act).astype(jnp.bfloat16)

    for c in range(chunks):
        for j in range(1, experts):
            dispatch(c, j).wait_send()

    def finish(c):
        pair(c).wait_recv()
        tot = own[c % 2] + pair_in[c]
        xg[c] = tot.astype(jnp.bfloat16)
        for j in range(1, experts):
            give_back(c, j).start()
        own_back(c).start()

    d_tile = dc // D_TILES
    for c in range(chunks):
        if c >= 2:
            pair(c - 2).wait_send()
        for d in range(D_TILES):
            cols = pl.ds(d * d_tile, d_tile)
            y = jnp.dot(hid[0], dw[c, :, cols], preferred_element_type=jnp.float32)
            dx = lax.dot_general(hid[1], gw[c, cols, :], NT, preferred_element_type=jnp.float32)
            dx = dx + lax.dot_general(
                hid[2], uw[c, cols, :], NT, preferred_element_type=jnp.float32
            )
            y = y.reshape(2, experts, CAP, d_tile)
            dx = dx.reshape(2, experts, CAP, d_tile)
            own[c % 2, :, :CAP, cols] = y[0]
            own[c % 2, :, CAP:, cols] = dx[0]
            pair_out[c % 2, :, :CAP, cols] = y[1]
            pair_out[c % 2, :, CAP:, cols] = dx[1]
        pair(c).start()
        if c >= 1:
            finish(c - 1)
    finish(chunks - 1)

    lane = lax.broadcasted_iota(jnp.int32, (toks, picks), 1)
    gwts_ref[...] = jnp.zeros_like(gwts_ref)

    @pl.loop(0, chunks)
    def _(c):
        cols = pl.ds(pl.multiple_of(c * dc, dc), dc)
        own_back(c).wait()
        for j in range(1, experts):
            give_back(c, j).wait_recv()
        both = ret[c].astype(jnp.float32)
        ys = both[:, :CAP, :].reshape(half, dc).astype(jnp.bfloat16)
        dxs = both[:, CAP:, :].reshape(half, dc).astype(jnp.bfloat16)
        picked = jnp.dot(placer, ys, preferred_element_type=jnp.float32)
        grad32 = cot_ref[:, cols].astype(jnp.float32)
        total = jnp.zeros((toks, dc), jnp.float32)
        dots = jnp.zeros((toks, picks), jnp.float32)
        for k in range(picks):
            pick = picked[k * toks : (k + 1) * toks]
            total = total + wts[:, k : k + 1] * pick
            dots = jnp.where(lane == k, jnp.sum(grad32 * pick, axis=1, keepdims=True), dots)
        gwts_ref[...] += dots
        mixed_ref[:, cols] = total.astype(jnp.bfloat16)
        gtok_ref[:, cols] = jnp.dot(
            placer_tok, dxs, preferred_element_type=jnp.float32
        ).astype(jnp.bfloat16)

    for c in range(chunks):
        forward(c).wait_send()
        if c >= chunks - 2:
            pair(c).wait_send()
        for j in range(1, experts):
            give_back(c, j).wait_send()


def fused_experts(experts, rows_in, exps, ids, wts, cot, gate_w, up_w, down_w):
    toks, width = rows_in.shape
    ff = gate_w.shape[1]
    c, dc, rows = CHUNKS, width // CHUNKS, 2 * experts * CAP
    dma = pltpu.SemaphoreType.DMA
    return pl.pallas_call(
        functools.partial(fused_kernel, experts),
        out_shape=(
            jax.ShapeDtypeStruct((toks, width), jnp.bfloat16),
            jax.ShapeDtypeStruct((toks, width), jnp.bfloat16),
            jax.ShapeDtypeStruct(ids.shape, jnp.float32),
        ),
        in_specs=[pl.BlockSpec(memory_space=pltpu.VMEM)] * 5
        + [pl.BlockSpec(memory_space=pl.ANY)] * 3,
        out_specs=[pl.BlockSpec(memory_space=pltpu.VMEM)] * 3,
        scratch_shapes=[
            pltpu.VMEM((c, experts, 2 * CAP, dc), jnp.bfloat16),
            pltpu.VMEM((c, experts, 2 * CAP, dc), jnp.bfloat16),
            pltpu.VMEM((c, dc, ff), jnp.bfloat16),
            pltpu.VMEM((c, dc, ff), jnp.bfloat16),
            pltpu.VMEM((c, ff, dc), jnp.bfloat16),
            pltpu.VMEM((c, 2, experts, 2 * CAP, dc), jnp.bfloat16),
            pltpu.VMEM((3, rows, ff), jnp.float32),
            pltpu.VMEM((3, rows, ff), jnp.bfloat16),
            pltpu.VMEM((2, experts, 2 * CAP, dc), jnp.float32),
            pltpu.VMEM((2, experts, 2 * CAP, dc), jnp.float32),
            pltpu.VMEM((c, experts, 2 * CAP, dc), jnp.float32),
            dma((3, c)),
            dma((c, experts)),
            dma((c, experts)),
            dma((c,)),
            dma((c,)),
            dma((c,)),
            dma((c,)),
            dma((c, experts)),
            dma((c, experts)),
        ],
        compiler_params=pltpu.CompilerParams(
            collective_id=0, has_side_effects=True, vmem_limit_bytes=63 * 2**20
        ),
        cost_estimate=pl.CostEstimate(
            flops=12 * rows * width * ff, bytes_accessed=6 * width * ff, transcendentals=rows * ff
        ),
    )(rows_in, exps, ids, wts, cot, gate_w, up_w, down_w)


def expert_pass(rows, grads, gate_w, up_w, down_w):
    gate = jnp.dot(rows, gate_w, preferred_element_type=jnp.float32)
    up = jnp.dot(rows, up_w, preferred_element_type=jnp.float32)
    sig = jax.nn.sigmoid(gate)
    act = gate * sig
    hidden = (act * up).astype(jnp.bfloat16)
    out_part = jnp.dot(hidden, down_w, preferred_element_type=jnp.float32)
    back = lax.dot_general(
        grads, down_w, (((1,), (1,)), ((), ())), preferred_element_type=jnp.float32
    )
    d_gate = (back * up * sig * (1.0 + gate * (1.0 - sig))).astype(jnp.bfloat16)
    d_up = (back * act).astype(jnp.bfloat16)
    in_part = lax.dot_general(
        d_gate, gate_w, (((1,), (1,)), ((), ())), preferred_element_type=jnp.float32
    )
    in_part = in_part + lax.dot_general(
        d_up, up_w, (((1,), (1,)), ((), ())), preferred_element_type=jnp.float32
    )
    return (out_part, in_part)


def exchange(send_x, send_g, gate_w, up_w, down_w, experts, pair, width):
    dup_x = jnp.broadcast_to(send_x[:, None], (experts, pair, CAP, width)).reshape(
        experts * pair, CAP, width
    )
    dup_g = jnp.broadcast_to(send_g[:, None], (experts, pair, CAP, width)).reshape(
        experts * pair, CAP, width
    )
    got_x, got_g = (
        lax.all_to_all(dup_x, ("expert", "tensor"), split_axis=0, concat_axis=0, tiled=True),
        lax.all_to_all(dup_g, ("expert", "tensor"), split_axis=0, concat_axis=0, tiled=True),
    )
    out_part, in_part = expert_pass(
        got_x.reshape(-1, width), got_g.reshape(-1, width), gate_w, up_w, down_w
    )
    back_y, back_dx = (
        lax.all_to_all(
            out_part.reshape(experts * pair, CAP, width),
            ("expert", "tensor"),
            split_axis=0,
            concat_axis=0,
            tiled=True,
        ),
        lax.all_to_all(
            in_part.reshape(experts * pair, CAP, width),
            ("expert", "tensor"),
            split_axis=0,
            concat_axis=0,
            tiled=True,
        ),
    )
    y_back = (
        jnp.sum(back_y.reshape(experts, pair, CAP, width), axis=1)
        .astype(jnp.bfloat16)
        .reshape(experts * CAP, width)
    )
    dx_back = (
        jnp.sum(back_dx.reshape(experts, pair, CAP, width), axis=1)
        .astype(jnp.bfloat16)
        .reshape(experts * CAP, width)
    )
    return (y_back, dx_back)


def body(
    quant_rows,
    block_exps,
    expert_ids,
    route_weights,
    gate_weight,
    up_weight,
    down_weight,
    cotangent,
):
    tok_rows, width = quant_rows.shape
    blocks = block_exps.shape[1]
    picks = expert_ids.shape[1]
    experts = lax.axis_size("expert")
    pair = lax.axis_size("tensor")
    if experts <= 8:
        return fused_experts(
            experts,
            quant_rows,
            block_exps,
            expert_ids,
            route_weights,
            cotangent,
            gate_weight[0],
            up_weight[0],
            down_weight[0],
        )
    scales = jnp.exp2(block_exps.astype(jnp.float32))
    tokens = (
        (
            quant_rows.astype(jnp.float32).reshape(tok_rows, blocks, width // blocks)
            * scales[:, :, None]
        )
        .reshape(tok_rows, width)
        .astype(jnp.bfloat16)
    )
    flat_ids = expert_ids.reshape(-1)
    onehot = (flat_ids[:, None] == jnp.arange(experts, dtype=jnp.int32)[None, :]).astype(jnp.int32)
    before = jnp.cumsum(onehot, axis=0) - onehot
    slot = jnp.sum(before * onehot, axis=1)
    target = flat_ids * CAP + slot
    placer = (jnp.arange(experts * CAP, dtype=jnp.int32)[:, None] == target[None, :]).astype(
        jnp.bfloat16
    )
    placer_tok = jnp.sum(
        placer.reshape(experts * CAP, tok_rows, picks).astype(jnp.float32), axis=2
    ).astype(jnp.bfloat16)
    grad32 = cotangent.astype(jnp.float32)
    scaled_grad = (
        (route_weights[:, :, None] * grad32[:, None, :])
        .astype(jnp.bfloat16)
        .reshape(tok_rows * picks, width)
    )
    send_x = (
        jnp.dot(placer_tok, tokens, preferred_element_type=jnp.float32)
        .astype(jnp.bfloat16)
        .reshape(experts, CAP, width)
    )
    send_g = (
        jnp.dot(placer, scaled_grad, preferred_element_type=jnp.float32)
        .astype(jnp.bfloat16)
        .reshape(experts, CAP, width)
    )
    gate_w = gate_weight[0]
    up_w = up_weight[0]
    down_w = down_weight[0]
    y_back, dx_back = exchange(send_x, send_g, gate_w, up_w, down_w, experts, pair, width)
    picked_y = lax.dot_general(
        placer, y_back, (((0,), (0,)), ((), ())), preferred_element_type=jnp.float32
    ).reshape(tok_rows, picks, width)
    picked_dx = lax.dot_general(
        placer, dx_back, (((0,), (0,)), ((), ())), preferred_element_type=jnp.float32
    ).reshape(tok_rows, picks, width)
    mixed = jnp.sum(route_weights[:, :, None] * picked_y, axis=1).astype(jnp.bfloat16)
    grad_tokens = jnp.sum(picked_dx, axis=1).astype(jnp.bfloat16)
    grad_weights = jnp.sum(grad32[:, None, :] * picked_y, axis=2)
    return (mixed, grad_tokens, grad_weights)


def solution(mesh):
    in_specs = (
        P(("groups", "expert", "tensor"), None),
        P(("groups", "expert", "tensor"), None),
        P(("groups", "expert", "tensor"), None),
        P(("groups", "expert", "tensor"), None),
        P("expert", None, "tensor"),
        P("expert", None, "tensor"),
        P("expert", "tensor", None),
        P(("groups", "expert", "tensor"), None),
    )
    out_specs = (
        P(("groups", "expert", "tensor"), None),
        P(("groups", "expert", "tensor"), None),
        P(("groups", "expert", "tensor"), None),
    )
    return jax.shard_map(body, mesh=mesh, in_specs=in_specs, out_specs=out_specs, check_vma=False)
```

```python
import functools

import jax
import jax.numpy as jnp
from jax import lax
from jax.experimental import pallas as pl
from jax.experimental.pallas import tpu as pltpu
from jax.sharding import PartitionSpec as P

CAP = 8

MESH = pl.DeviceIdType.MESH
NT = (((1,), (1,)), ((), ()))
TN = (((0,), (0,)), ((), ()))
BLOCK = 128
CHUNKS = 6
F_TILES = 3
D_TILES = 2
E_TILES = 7


def fused_kernel(
    experts,
    q_ref,
    exp_ref,
    ids_ref,
    wts_ref,
    cot_ref,
    gate_hbm,
    up_hbm,
    down_hbm,
    rows_ref,
    gwts_ref,
    xg,
    ret,
    gw,
    uw,
    dw,
    rx,
    acc,
    hid,
    own,
    pair_out,
    pair_in,
    w_sem,
    d_send,
    d_recv,
    f_send,
    f_recv,
    p_send,
    p_recv,
    r_send,
    r_recv,
):
    chunks, dc, ff = gw.shape
    half = experts * CAP
    me = lax.axis_index("expert")
    core = lax.axis_index("tensor")
    mate = {"tensor": 1 - core}

    def weight_copies(c):
        cols = pl.ds(pl.multiple_of(c * dc, dc), dc)
        return (
            pltpu.make_async_copy(gate_hbm.at[cols, :], gw.at[c], w_sem.at[0, c]),
            pltpu.make_async_copy(up_hbm.at[cols, :], uw.at[c], w_sem.at[1, c]),
            pltpu.make_async_copy(down_hbm.at[:, cols], dw.at[c], w_sem.at[2, c]),
        )

    def own_copy(c):
        return pltpu.make_async_copy(
            xg.at[c, me], rx.at[c, 0, 0], d_recv.at[c, 0]
        )

    def dispatch(c, j):
        peer = lax.rem(me + j, experts)
        return pltpu.make_async_remote_copy(
            src_ref=xg.at[c, peer],
            dst_ref=rx.at[c, 0, j],
            send_sem=d_send.at[c, j],
            recv_sem=d_recv.at[c, j],
            device_id={"expert": peer},
            device_id_type=MESH,
        )

    def forward(c):
        return pltpu.make_async_remote_copy(
            src_ref=rx.at[c, 0],
            dst_ref=rx.at[c, 1],
            send_sem=f_send.at[c],
            recv_sem=f_recv.at[c],
            device_id=mate,
            device_id_type=MESH,
        )

    def pair(c):
        return pltpu.make_async_remote_copy(
            src_ref=pair_out.at[c % 2],
            dst_ref=pair_in.at[c],
            send_sem=p_send.at[c],
            recv_sem=p_recv.at[c],
            device_id=mate,
            device_id_type=MESH,
        )

    def own_back(c):
        return pltpu.make_async_copy(
            xg.at[c, 0], ret.at[c, me], r_recv.at[c, 0]
        )

    def give_back(c, j):
        return pltpu.make_async_remote_copy(
            src_ref=xg.at[c, j],
            dst_ref=ret.at[c, me],
            send_sem=r_send.at[c, j],
            recv_sem=r_recv.at[c, j],
            device_id={"expert": lax.rem(me + experts - j, experts)},
            device_id_type=MESH,
        )

    for c in range(chunks):
        for copy in weight_copies(c):
            copy.start()

    picks, toks = ids_ref.shape
    later = lax.broadcasted_iota(jnp.int32, (toks, toks), 0)
    earlier = lax.broadcasted_iota(jnp.int32, (toks, toks), 1)

    def column(row):
        return jnp.sum(jnp.where(later == earlier, row, 0.0), axis=1, keepdims=True)

    ids = [column(ids_ref[k : k + 1, :].astype(jnp.float32)) for k in range(picks)]
    wts = [column(wts_ref[k : k + 1, :]) for k in range(picks)]
    place = lax.broadcasted_iota(jnp.int32, (toks, half), 1)
    expert_of = (place // CAP).astype(jnp.float32)
    hits = [(ids[k] == expert_of).astype(jnp.float32) for k in range(picks)]
    named = hits[0]
    for k in range(1, picks):
        named = named + hits[k]
    below = (earlier < later).astype(jnp.bfloat16)
    before = jnp.dot(below, named.astype(jnp.bfloat16), preferred_element_type=jnp.float32)
    in_slot = (before == (place % CAP).astype(jnp.float32)).astype(jnp.float32)
    placer = jnp.concatenate([hit * in_slot for hit in hits], axis=0).astype(jnp.bfloat16)
    placer_tok = (named * in_slot).astype(jnp.bfloat16)
    exps = exp_ref[...]
    scales = jnp.where(
        exps >= 0, jnp.where(exps == 1, 2.0, 1.0), jnp.where(exps == -1, 0.5, 0.25)
    ).astype(jnp.float32)

    def prepare(c):
        parts = []
        for b in range(c * dc // BLOCK, (c + 1) * dc // BLOCK):
            part = q_ref[:, b * BLOCK : (b + 1) * BLOCK].astype(jnp.float32)
            parts.append((part * scales[:, b : b + 1]).astype(jnp.bfloat16))
        toks_c = jnp.concatenate(parts, axis=1)
        grad32 = cot_ref[:, pl.ds(c * dc, dc)].astype(jnp.float32)
        scaled = jnp.concatenate([wts[k] * grad32 for k in range(picks)], axis=0)
        xs = lax.dot_general(placer_tok, toks_c, TN, preferred_element_type=jnp.float32)
        gs = lax.dot_general(
            placer, scaled.astype(jnp.bfloat16), TN, preferred_element_type=jnp.float32
        )
        both = [xs.reshape(experts, CAP, dc), gs.reshape(experts, CAP, dc)]
        xg[c] = jnp.concatenate(both, axis=1).astype(jnp.bfloat16)

    prepare(0)
    barrier = pltpu.get_barrier_semaphore()
    for j in range(1, experts):
        pl.semaphore_signal(
            barrier,
            inc=1,
            device_id={"expert": lax.rem(me + j, experts)},
            device_id_type=MESH,
        )
    pl.semaphore_signal(barrier, inc=1, device_id=mate, device_id_type=MESH)
    pl.semaphore_wait(barrier, experts)

    for c in range(chunks):
        if c > 0:
            prepare(c)
        own_copy(c).start()
        for j in range(1, experts):
            dispatch(c, j).start()
    def collect(c):
        own_copy(c).wait()
        for j in range(1, experts):
            dispatch(c, j).wait_recv()
        forward(c).start()

    f_tile = ff // F_TILES
    def project(c):
        forward(c).wait_recv()
        for copy in weight_copies(c):
            copy.wait()
        both = rx[c].astype(jnp.float32)
        xs = both[:, :, :CAP, :].reshape(2 * half, dc).astype(jnp.bfloat16)
        gs = both[:, :, CAP:, :].reshape(2 * half, dc).astype(jnp.bfloat16)
        for f in range(F_TILES):
            cols = pl.ds(f * f_tile, f_tile)
            gate = jnp.dot(xs, gw[c, :, cols], preferred_element_type=jnp.float32)
            up = jnp.dot(xs, uw[c, :, cols], preferred_element_type=jnp.float32)
            back = lax.dot_general(gs, dw[c, cols, :], NT, preferred_element_type=jnp.float32)
            acc[0, :, cols] += gate
            acc[1, :, cols] += up
            acc[2, :, cols] += back
            if f == 0:

                @pl.when(c + 1 < chunks)
                def _():
                    collect(c + 1)

    acc[...] = jnp.zeros_like(acc)
    collect(0)

    @pl.loop(0, chunks)
    def _(c):
        project(c)

    e_tile = ff // E_TILES
    for e in range(E_TILES):
        cols = pl.ds(e * e_tile, e_tile)
        gate = acc[0, :, cols]
        up = acc[1, :, cols]
        back = acc[2, :, cols]
        sig = jax.nn.sigmoid(gate)
        act = gate * sig
        hid[0, :, cols] = (act * up).astype(jnp.bfloat16)
        hid[1, :, cols] = (back * up * sig * (1.0 + gate * (1.0 - sig))).astype(jnp.bfloat16)
        hid[2, :, cols] = (back * act).astype(jnp.bfloat16)

    for c in range(chunks):
        for j in range(1, experts):
            dispatch(c, j).wait_send()

    def finish(c):
        pair(c).wait_recv()
        tot = own[c % 2] + pair_in[c]
        xg[c] = tot.astype(jnp.bfloat16)
        for j in range(1, experts):
            give_back(c, j).start()
        own_back(c).start()

    d_tile = dc // D_TILES
    for c in range(chunks):
        if c >= 2:
            pair(c - 2).wait_send()
        for d in range(D_TILES):
            cols = pl.ds(d * d_tile, d_tile)
            y = jnp.dot(hid[0], dw[c, :, cols], preferred_element_type=jnp.float32)
            dx = lax.dot_general(hid[1], gw[c, cols, :], NT, preferred_element_type=jnp.float32)
            dx = dx + lax.dot_general(
                hid[2], uw[c, cols, :], NT, preferred_element_type=jnp.float32
            )
            y = y.reshape(2, experts, CAP, d_tile)
            dx = dx.reshape(2, experts, CAP, d_tile)
            own[c % 2, :, :CAP, cols] = y[0]
            own[c % 2, :, CAP:, cols] = dx[0]
            pair_out[c % 2, :, :CAP, cols] = y[1]
            pair_out[c % 2, :, CAP:, cols] = dx[1]
            if c >= 1 and d == 0:
                finish(c - 1)
        pair(c).start()
    finish(chunks - 1)

    gwts_ref[...] = jnp.zeros_like(gwts_ref)

    @pl.loop(0, chunks)
    def _(c):
        cols = pl.ds(pl.multiple_of(c * dc, dc), dc)
        own_back(c).wait()
        for j in range(1, experts):
            give_back(c, j).wait_recv()
        both = ret[c].astype(jnp.float32)
        ys = both[:, :CAP, :].reshape(half, dc).astype(jnp.bfloat16)
        dxs = both[:, CAP:, :].reshape(half, dc).astype(jnp.bfloat16)
        picked = jnp.dot(placer, ys, preferred_element_type=jnp.float32)
        grad32 = cot_ref[:, cols].astype(jnp.float32)
        total = jnp.zeros((toks, dc), jnp.float32)
        dots = []
        for k in range(picks):
            pick = picked[k * toks : (k + 1) * toks]
            total = total + wts[k] * pick
            dot = jnp.sum(grad32 * pick, axis=1, keepdims=True)
            dots.append(jnp.sum(jnp.where(later == earlier, dot, 0.0), axis=0, keepdims=True))
        gwts_ref[...] += jnp.concatenate(dots, axis=0)
        rows_ref[0, :, cols] = total
        rows_ref[1, :, cols] = jnp.dot(placer_tok, dxs, preferred_element_type=jnp.float32)

    for c in range(chunks):
        forward(c).wait_send()
        if c >= chunks - 2:
            pair(c).wait_send()
        for j in range(1, experts):
            give_back(c, j).wait_send()


def fused_experts(experts, rows_in, exps, ids, wts, cot, gate_w, up_w, down_w):
    toks, width = rows_in.shape
    ff = gate_w.shape[1]
    c, dc, slots = CHUNKS, width // CHUNKS, 2 * experts * CAP
    dma = pltpu.SemaphoreType.DMA
    rows, gwts = pl.pallas_call(
        functools.partial(fused_kernel, experts),
        out_shape=(
            jax.ShapeDtypeStruct((2, toks, width), jnp.float32),
            jax.ShapeDtypeStruct(ids.shape, jnp.float32),
        ),
        in_specs=[pl.BlockSpec(memory_space=pltpu.VMEM)] * 5
        + [pl.BlockSpec(memory_space=pl.ANY)] * 3,
        out_specs=[pl.BlockSpec(memory_space=pltpu.VMEM)] * 2,
        scratch_shapes=[
            pltpu.VMEM((c, experts, 2 * CAP, dc), jnp.bfloat16),
            pltpu.VMEM((c, experts, 2 * CAP, dc), jnp.bfloat16),
            pltpu.VMEM((c, dc, ff), jnp.bfloat16),
            pltpu.VMEM((c, dc, ff), jnp.bfloat16),
            pltpu.VMEM((c, ff, dc), jnp.bfloat16),
            pltpu.VMEM((c, 2, experts, 2 * CAP, dc), jnp.bfloat16),
            pltpu.VMEM((3, slots, ff), jnp.float32),
            pltpu.VMEM((3, slots, ff), jnp.bfloat16),
            pltpu.VMEM((2, experts, 2 * CAP, dc), jnp.float32),
            pltpu.VMEM((2, experts, 2 * CAP, dc), jnp.float32),
            pltpu.VMEM((c, experts, 2 * CAP, dc), jnp.float32),
            dma((3, c)),
            dma((c, experts)),
            dma((c, experts)),
            dma((c,)),
            dma((c,)),
            dma((c,)),
            dma((c,)),
            dma((c, experts)),
            dma((c, experts)),
        ],
        compiler_params=pltpu.CompilerParams(
            collective_id=0, has_side_effects=True, vmem_limit_bytes=63 * 2**20
        ),
        cost_estimate=pl.CostEstimate(
            flops=12 * slots * width * ff, bytes_accessed=6 * width * ff, transcendentals=slots * ff
        ),
    )(rows_in, exps, ids, wts, cot, gate_w, up_w, down_w)
    return (rows[0].astype(jnp.bfloat16), rows[1].astype(jnp.bfloat16), gwts.T)


def expert_pass(rows, grads, gate_w, up_w, down_w):
    gate = jnp.dot(rows, gate_w, preferred_element_type=jnp.float32)
    up = jnp.dot(rows, up_w, preferred_element_type=jnp.float32)
    sig = jax.nn.sigmoid(gate)
    act = gate * sig
    hidden = (act * up).astype(jnp.bfloat16)
    out_part = jnp.dot(hidden, down_w, preferred_element_type=jnp.float32)
    back = lax.dot_general(
        grads, down_w, (((1,), (1,)), ((), ())), preferred_element_type=jnp.float32
    )
    d_gate = (back * up * sig * (1.0 + gate * (1.0 - sig))).astype(jnp.bfloat16)
    d_up = (back * act).astype(jnp.bfloat16)
    in_part = lax.dot_general(
        d_gate, gate_w, (((1,), (1,)), ((), ())), preferred_element_type=jnp.float32
    )
    in_part = in_part + lax.dot_general(
        d_up, up_w, (((1,), (1,)), ((), ())), preferred_element_type=jnp.float32
    )
    return (out_part, in_part)


def exchange(send_x, send_g, gate_w, up_w, down_w, experts, pair, width):
    dup_x = jnp.broadcast_to(send_x[:, None], (experts, pair, CAP, width)).reshape(
        experts * pair, CAP, width
    )
    dup_g = jnp.broadcast_to(send_g[:, None], (experts, pair, CAP, width)).reshape(
        experts * pair, CAP, width
    )
    got_x, got_g = (
        lax.all_to_all(dup_x, ("expert", "tensor"), split_axis=0, concat_axis=0, tiled=True),
        lax.all_to_all(dup_g, ("expert", "tensor"), split_axis=0, concat_axis=0, tiled=True),
    )
    out_part, in_part = expert_pass(
        got_x.reshape(-1, width), got_g.reshape(-1, width), gate_w, up_w, down_w
    )
    back_y, back_dx = (
        lax.all_to_all(
            out_part.reshape(experts * pair, CAP, width),
            ("expert", "tensor"),
            split_axis=0,
            concat_axis=0,
            tiled=True,
        ),
        lax.all_to_all(
            in_part.reshape(experts * pair, CAP, width),
            ("expert", "tensor"),
            split_axis=0,
            concat_axis=0,
            tiled=True,
        ),
    )
    y_back = (
        jnp.sum(back_y.reshape(experts, pair, CAP, width), axis=1)
        .astype(jnp.bfloat16)
        .reshape(experts * CAP, width)
    )
    dx_back = (
        jnp.sum(back_dx.reshape(experts, pair, CAP, width), axis=1)
        .astype(jnp.bfloat16)
        .reshape(experts * CAP, width)
    )
    return (y_back, dx_back)


def body(
    quant_rows,
    block_exps,
    expert_ids,
    route_weights,
    gate_weight,
    up_weight,
    down_weight,
    cotangent,
):
    tok_rows, width = quant_rows.shape
    blocks = block_exps.shape[1]
    picks = expert_ids.shape[1]
    experts = lax.axis_size("expert")
    pair = lax.axis_size("tensor")
    if experts <= 8:
        return fused_experts(
            experts,
            quant_rows,
            block_exps,
            expert_ids.T,
            route_weights.T,
            cotangent,
            gate_weight[0],
            up_weight[0],
            down_weight[0],
        )
    scales = jnp.exp2(block_exps.astype(jnp.float32))
    tokens = (
        (
            quant_rows.astype(jnp.float32).reshape(tok_rows, blocks, width // blocks)
            * scales[:, :, None]
        )
        .reshape(tok_rows, width)
        .astype(jnp.bfloat16)
    )
    flat_ids = expert_ids.reshape(-1)
    onehot = (flat_ids[:, None] == jnp.arange(experts, dtype=jnp.int32)[None, :]).astype(jnp.int32)
    before = jnp.cumsum(onehot, axis=0) - onehot
    slot = jnp.sum(before * onehot, axis=1)
    target = flat_ids * CAP + slot
    placer = (jnp.arange(experts * CAP, dtype=jnp.int32)[:, None] == target[None, :]).astype(
        jnp.bfloat16
    )
    placer_tok = jnp.sum(
        placer.reshape(experts * CAP, tok_rows, picks).astype(jnp.float32), axis=2
    ).astype(jnp.bfloat16)
    grad32 = cotangent.astype(jnp.float32)
    scaled_grad = (
        (route_weights[:, :, None] * grad32[:, None, :])
        .astype(jnp.bfloat16)
        .reshape(tok_rows * picks, width)
    )
    send_x = (
        jnp.dot(placer_tok, tokens, preferred_element_type=jnp.float32)
        .astype(jnp.bfloat16)
        .reshape(experts, CAP, width)
    )
    send_g = (
        jnp.dot(placer, scaled_grad, preferred_element_type=jnp.float32)
        .astype(jnp.bfloat16)
        .reshape(experts, CAP, width)
    )
    gate_w = gate_weight[0]
    up_w = up_weight[0]
    down_w = down_weight[0]
    y_back, dx_back = exchange(send_x, send_g, gate_w, up_w, down_w, experts, pair, width)
    picked_y = lax.dot_general(
        placer, y_back, (((0,), (0,)), ((), ())), preferred_element_type=jnp.float32
    ).reshape(tok_rows, picks, width)
    picked_dx = lax.dot_general(
        placer, dx_back, (((0,), (0,)), ((), ())), preferred_element_type=jnp.float32
    ).reshape(tok_rows, picks, width)
    mixed = jnp.sum(route_weights[:, :, None] * picked_y, axis=1).astype(jnp.bfloat16)
    grad_tokens = jnp.sum(picked_dx, axis=1).astype(jnp.bfloat16)
    grad_weights = jnp.sum(grad32[:, None, :] * picked_y, axis=2)
    return (mixed, grad_tokens, grad_weights)


def solution(mesh):
    in_specs = (
        P(("groups", "expert", "tensor"), None),
        P(("groups", "expert", "tensor"), None),
        P(("groups", "expert", "tensor"), None),
        P(("groups", "expert", "tensor"), None),
        P("expert", None, "tensor"),
        P("expert", None, "tensor"),
        P("expert", "tensor", None),
        P(("groups", "expert", "tensor"), None),
    )
    out_specs = (
        P(("groups", "expert", "tensor"), None),
        P(("groups", "expert", "tensor"), None),
        P(("groups", "expert", "tensor"), None),
    )
    return jax.shard_map(body, mesh=mesh, in_specs=in_specs, out_specs=out_specs, check_vma=False)
```

```python
import functools

import jax
import jax.numpy as jnp
from jax import lax
from jax.experimental import pallas as pl
from jax.experimental.pallas import tpu as pltpu
from jax.sharding import PartitionSpec as P

CAP = 8

MESH = pl.DeviceIdType.MESH
NT = (((1,), (1,)), ((), ()))
TN = (((0,), (0,)), ((), ()))
BLOCK = 128
CHUNKS = 6
F_TILES = 3
D_TILES = 2
E_TILES = 7


def fused_kernel(
    experts,
    q_ref,
    exp_ref,
    ids_ref,
    wts_ref,
    cot_ref,
    gate_hbm,
    up_hbm,
    down_hbm,
    rows_ref,
    gwts_ref,
    xg,
    ret,
    gw,
    uw,
    dw,
    rx,
    acc,
    hid,
    own,
    pair_out,
    pair_in,
    w_sem,
    d_send,
    d_recv,
    f_send,
    f_recv,
    p_send,
    p_recv,
    r_send,
    r_recv,
):
    chunks, dc, ff = gw.shape
    half = experts * CAP
    me = lax.axis_index("expert")
    core = lax.axis_index("tensor")
    mate = {"tensor": 1 - core}

    def weight_copies(c):
        cols = pl.ds(pl.multiple_of(c * dc, dc), dc)
        return (
            pltpu.make_async_copy(gate_hbm.at[cols, :], gw.at[c], w_sem.at[0, c]),
            pltpu.make_async_copy(up_hbm.at[cols, :], uw.at[c], w_sem.at[1, c]),
            pltpu.make_async_copy(down_hbm.at[:, cols], dw.at[c], w_sem.at[2, c]),
        )

    def own_copy(c):
        return pltpu.make_async_copy(
            xg.at[c, me], rx.at[c, 0, 0], d_recv.at[c, 0]
        )

    def dispatch(c, j):
        peer = lax.rem(me + j, experts)
        return pltpu.make_async_remote_copy(
            src_ref=xg.at[c, peer],
            dst_ref=rx.at[c, 0, j],
            send_sem=d_send.at[c, j],
            recv_sem=d_recv.at[c, j],
            device_id={"expert": peer},
            device_id_type=MESH,
        )

    def forward(c):
        return pltpu.make_async_remote_copy(
            src_ref=rx.at[c, 0],
            dst_ref=rx.at[c, 1],
            send_sem=f_send.at[c],
            recv_sem=f_recv.at[c],
            device_id=mate,
            device_id_type=MESH,
        )

    def pair(c):
        return pltpu.make_async_remote_copy(
            src_ref=pair_out.at[c % 2],
            dst_ref=pair_in.at[c],
            send_sem=p_send.at[c],
            recv_sem=p_recv.at[c],
            device_id=mate,
            device_id_type=MESH,
        )

    def own_back(c):
        return pltpu.make_async_copy(
            xg.at[c, 0], ret.at[c, me], r_recv.at[c, 0]
        )

    def give_back(c, j):
        return pltpu.make_async_remote_copy(
            src_ref=xg.at[c, j],
            dst_ref=ret.at[c, me],
            send_sem=r_send.at[c, j],
            recv_sem=r_recv.at[c, j],
            device_id={"expert": lax.rem(me + experts - j, experts)},
            device_id_type=MESH,
        )

    for c in range(chunks):
        for copy in weight_copies(c):
            copy.start()

    picks, toks = ids_ref.shape
    later = lax.broadcasted_iota(jnp.int32, (toks, toks), 0)
    earlier = lax.broadcasted_iota(jnp.int32, (toks, toks), 1)

    def column(row):
        return jnp.sum(jnp.where(later == earlier, row, 0.0), axis=1, keepdims=True)

    ids = [column(ids_ref[k : k + 1, :].astype(jnp.float32)) for k in range(picks)]
    wts = [column(wts_ref[k : k + 1, :]) for k in range(picks)]
    place = lax.broadcasted_iota(jnp.int32, (toks, half), 1)
    expert_of = (place // CAP).astype(jnp.float32)
    hits = [(ids[k] == expert_of).astype(jnp.float32) for k in range(picks)]
    named = hits[0]
    for k in range(1, picks):
        named = named + hits[k]
    below = (earlier < later).astype(jnp.bfloat16)
    before = jnp.dot(below, named.astype(jnp.bfloat16), preferred_element_type=jnp.float32)
    in_slot = (before == (place % CAP).astype(jnp.float32)).astype(jnp.float32)
    placer = jnp.concatenate([hit * in_slot for hit in hits], axis=0).astype(jnp.bfloat16)
    placer_tok = (named * in_slot).astype(jnp.bfloat16)
    exps = exp_ref[...]
    scales = jnp.where(
        exps >= 0, jnp.where(exps == 1, 2.0, 1.0), jnp.where(exps == -1, 0.5, 0.25)
    ).astype(jnp.float32)

    def prepare(c):
        parts = []
        for b in range(c * dc // BLOCK, (c + 1) * dc // BLOCK):
            part = q_ref[:, b * BLOCK : (b + 1) * BLOCK].astype(jnp.float32)
            parts.append((part * scales[:, b : b + 1]).astype(jnp.bfloat16))
        toks_c = jnp.concatenate(parts, axis=1)
        grad32 = cot_ref[:, pl.ds(c * dc, dc)].astype(jnp.float32)
        scaled = jnp.concatenate([wts[k] * grad32 for k in range(picks)], axis=0)
        xs = lax.dot_general(placer_tok, toks_c, TN, preferred_element_type=jnp.float32)
        gs = lax.dot_general(
            placer, scaled.astype(jnp.bfloat16), TN, preferred_element_type=jnp.float32
        )
        both = [xs.reshape(experts, CAP, dc), gs.reshape(experts, CAP, dc)]
        xg[c] = jnp.concatenate(both, axis=1).astype(jnp.bfloat16)

    prepare(0)
    barrier = pltpu.get_barrier_semaphore()
    for j in range(1, experts):
        pl.semaphore_signal(
            barrier,
            inc=1,
            device_id={"expert": lax.rem(me + j, experts)},
            device_id_type=MESH,
        )
    pl.semaphore_signal(barrier, inc=1, device_id=mate, device_id_type=MESH)
    pl.semaphore_wait(barrier, experts)

    for c in range(chunks):
        if c > 0:
            prepare(c)
        own_copy(c).start()
        for j in range(1, experts):
            dispatch(c, j).start()
    def collect(c):
        own_copy(c).wait()
        for j in range(1, experts):
            dispatch(c, j).wait_recv()
        forward(c).start()

    f_tile = ff // F_TILES
    def project(c):
        forward(c).wait_recv()
        for copy in weight_copies(c):
            copy.wait()
        both = rx[c].astype(jnp.float32)
        xs = both[:, :, :CAP, :].reshape(2 * half, dc).astype(jnp.bfloat16)
        gs = both[:, :, CAP:, :].reshape(2 * half, dc).astype(jnp.bfloat16)
        for f in range(F_TILES):
            cols = pl.ds(f * f_tile, f_tile)
            gate = jnp.dot(xs, gw[c, :, cols], preferred_element_type=jnp.float32)
            up = jnp.dot(xs, uw[c, :, cols], preferred_element_type=jnp.float32)
            back = lax.dot_general(gs, dw[c, cols, :], NT, preferred_element_type=jnp.float32)
            acc[0, :, cols] += gate
            acc[1, :, cols] += up
            acc[2, :, cols] += back

    acc[...] = jnp.zeros_like(acc)
    collect(0)

    @pl.loop(0, chunks)
    def _(c):
        @pl.when(c + 1 < chunks)
        def _():
            collect(c + 1)

        project(c)

    e_tile = ff // E_TILES
    for e in range(E_TILES):
        cols = pl.ds(e * e_tile, e_tile)
        gate = acc[0, :, cols]
        up = acc[1, :, cols]
        back = acc[2, :, cols]
        sig = jax.nn.sigmoid(gate)
        act = gate * sig
        hid[0, :, cols] = (act * up).astype(jnp.bfloat16)
        hid[1, :, cols] = (back * up * sig * (1.0 + gate * (1.0 - sig))).astype(jnp.bfloat16)
        hid[2, :, cols] = (back * act).astype(jnp.bfloat16)

    for c in range(chunks):
        for j in range(1, experts):
            dispatch(c, j).wait_send()

    def finish(c):
        pair(c).wait_recv()
        tot = own[c % 2] + pair_in[c]
        xg[c] = tot.astype(jnp.bfloat16)
        for j in range(1, experts):
            give_back(c, j).start()
        own_back(c).start()

    d_tile = dc // D_TILES
    for c in range(chunks):
        if c >= 2:
            pair(c - 2).wait_send()
        for d in range(D_TILES):
            cols = pl.ds(d * d_tile, d_tile)
            y = jnp.dot(hid[0], dw[c, :, cols], preferred_element_type=jnp.float32)
            dx = lax.dot_general(hid[1], gw[c, cols, :], NT, preferred_element_type=jnp.float32)
            dx = dx + lax.dot_general(
                hid[2], uw[c, cols, :], NT, preferred_element_type=jnp.float32
            )
            y = y.reshape(2, experts, CAP, d_tile)
            dx = dx.reshape(2, experts, CAP, d_tile)
            own[c % 2, :, :CAP, cols] = y[0]
            own[c % 2, :, CAP:, cols] = dx[0]
            pair_out[c % 2, :, :CAP, cols] = y[1]
            pair_out[c % 2, :, CAP:, cols] = dx[1]
        pair(c).start()
        if c >= 1:
            finish(c - 1)
    finish(chunks - 1)

    gwts_ref[...] = jnp.zeros_like(gwts_ref)

    @pl.loop(0, chunks)
    def _(c):
        cols = pl.ds(pl.multiple_of(c * dc, dc), dc)
        own_back(c).wait()
        for j in range(1, experts):
            give_back(c, j).wait_recv()
        both = ret[c].astype(jnp.float32)
        ys = both[:, :CAP, :].reshape(half, dc).astype(jnp.bfloat16)
        dxs = both[:, CAP:, :].reshape(half, dc).astype(jnp.bfloat16)
        picked = jnp.dot(placer, ys, preferred_element_type=jnp.float32)
        grad32 = cot_ref[:, cols].astype(jnp.float32)
        total = jnp.zeros((toks, dc), jnp.float32)
        dots = []
        for k in range(picks):
            pick = picked[k * toks : (k + 1) * toks]
            total = total + wts[k] * pick
            dot = jnp.sum(grad32 * pick, axis=1, keepdims=True)
            dots.append(jnp.sum(jnp.where(later == earlier, dot, 0.0), axis=0, keepdims=True))
        gwts_ref[...] += jnp.concatenate(dots, axis=0)
        rows_ref[0, :, cols] = total
        rows_ref[1, :, cols] = jnp.dot(placer_tok, dxs, preferred_element_type=jnp.float32)

    for c in range(chunks):
        forward(c).wait_send()
        if c >= chunks - 2:
            pair(c).wait_send()
        for j in range(1, experts):
            give_back(c, j).wait_send()


def fused_experts(experts, rows_in, exps, ids, wts, cot, gate_w, up_w, down_w):
    toks, width = rows_in.shape
    ff = gate_w.shape[1]
    c, dc, slots = CHUNKS, width // CHUNKS, 2 * experts * CAP
    dma = pltpu.SemaphoreType.DMA
    rows, gwts = pl.pallas_call(
        functools.partial(fused_kernel, experts),
        out_shape=(
            jax.ShapeDtypeStruct((2, toks, width), jnp.float32),
            jax.ShapeDtypeStruct(ids.shape, jnp.float32),
        ),
        in_specs=[pl.BlockSpec(memory_space=pltpu.VMEM)] * 5
        + [pl.BlockSpec(memory_space=pl.ANY)] * 3,
        out_specs=[pl.BlockSpec(memory_space=pltpu.VMEM)] * 2,
        scratch_shapes=[
            pltpu.VMEM((c, experts, 2 * CAP, dc), jnp.bfloat16),
            pltpu.VMEM((c, experts, 2 * CAP, dc), jnp.bfloat16),
            pltpu.VMEM((c, dc, ff), jnp.bfloat16),
            pltpu.VMEM((c, dc, ff), jnp.bfloat16),
            pltpu.VMEM((c, ff, dc), jnp.bfloat16),
            pltpu.VMEM((c, 2, experts, 2 * CAP, dc), jnp.bfloat16),
            pltpu.VMEM((3, slots, ff), jnp.float32),
            pltpu.VMEM((3, slots, ff), jnp.bfloat16),
            pltpu.VMEM((2, experts, 2 * CAP, dc), jnp.float32),
            pltpu.VMEM((2, experts, 2 * CAP, dc), jnp.float32),
            pltpu.VMEM((c, experts, 2 * CAP, dc), jnp.float32),
            dma((3, c)),
            dma((c, experts)),
            dma((c, experts)),
            dma((c,)),
            dma((c,)),
            dma((c,)),
            dma((c,)),
            dma((c, experts)),
            dma((c, experts)),
        ],
        compiler_params=pltpu.CompilerParams(
            collective_id=0, has_side_effects=True, vmem_limit_bytes=63 * 2**20
        ),
        cost_estimate=pl.CostEstimate(
            flops=12 * slots * width * ff, bytes_accessed=6 * width * ff, transcendentals=slots * ff
        ),
    )(rows_in, exps, ids, wts, cot, gate_w, up_w, down_w)
    return (rows[0].astype(jnp.bfloat16), rows[1].astype(jnp.bfloat16), gwts.T)


def expert_pass(rows, grads, gate_w, up_w, down_w):
    gate = jnp.dot(rows, gate_w, preferred_element_type=jnp.float32)
    up = jnp.dot(rows, up_w, preferred_element_type=jnp.float32)
    sig = jax.nn.sigmoid(gate)
    act = gate * sig
    hidden = (act * up).astype(jnp.bfloat16)
    out_part = jnp.dot(hidden, down_w, preferred_element_type=jnp.float32)
    back = lax.dot_general(
        grads, down_w, (((1,), (1,)), ((), ())), preferred_element_type=jnp.float32
    )
    d_gate = (back * up * sig * (1.0 + gate * (1.0 - sig))).astype(jnp.bfloat16)
    d_up = (back * act).astype(jnp.bfloat16)
    in_part = lax.dot_general(
        d_gate, gate_w, (((1,), (1,)), ((), ())), preferred_element_type=jnp.float32
    )
    in_part = in_part + lax.dot_general(
        d_up, up_w, (((1,), (1,)), ((), ())), preferred_element_type=jnp.float32
    )
    return (out_part, in_part)


def exchange(send_x, send_g, gate_w, up_w, down_w, experts, pair, width):
    dup_x = jnp.broadcast_to(send_x[:, None], (experts, pair, CAP, width)).reshape(
        experts * pair, CAP, width
    )
    dup_g = jnp.broadcast_to(send_g[:, None], (experts, pair, CAP, width)).reshape(
        experts * pair, CAP, width
    )
    got_x, got_g = (
        lax.all_to_all(dup_x, ("expert", "tensor"), split_axis=0, concat_axis=0, tiled=True),
        lax.all_to_all(dup_g, ("expert", "tensor"), split_axis=0, concat_axis=0, tiled=True),
    )
    out_part, in_part = expert_pass(
        got_x.reshape(-1, width), got_g.reshape(-1, width), gate_w, up_w, down_w
    )
    back_y, back_dx = (
        lax.all_to_all(
            out_part.reshape(experts * pair, CAP, width),
            ("expert", "tensor"),
            split_axis=0,
            concat_axis=0,
            tiled=True,
        ),
        lax.all_to_all(
            in_part.reshape(experts * pair, CAP, width),
            ("expert", "tensor"),
            split_axis=0,
            concat_axis=0,
            tiled=True,
        ),
    )
    y_back = (
        jnp.sum(back_y.reshape(experts, pair, CAP, width), axis=1)
        .astype(jnp.bfloat16)
        .reshape(experts * CAP, width)
    )
    dx_back = (
        jnp.sum(back_dx.reshape(experts, pair, CAP, width), axis=1)
        .astype(jnp.bfloat16)
        .reshape(experts * CAP, width)
    )
    return (y_back, dx_back)


def body(
    quant_rows,
    block_exps,
    expert_ids,
    route_weights,
    gate_weight,
    up_weight,
    down_weight,
    cotangent,
):
    tok_rows, width = quant_rows.shape
    blocks = block_exps.shape[1]
    picks = expert_ids.shape[1]
    experts = lax.axis_size("expert")
    pair = lax.axis_size("tensor")
    if experts <= 8:
        return fused_experts(
            experts,
            quant_rows,
            block_exps,
            expert_ids.T,
            route_weights.T,
            cotangent,
            gate_weight[0],
            up_weight[0],
            down_weight[0],
        )
    scales = jnp.exp2(block_exps.astype(jnp.float32))
    tokens = (
        (
            quant_rows.astype(jnp.float32).reshape(tok_rows, blocks, width // blocks)
            * scales[:, :, None]
        )
        .reshape(tok_rows, width)
        .astype(jnp.bfloat16)
    )
    flat_ids = expert_ids.reshape(-1)
    onehot = (flat_ids[:, None] == jnp.arange(experts, dtype=jnp.int32)[None, :]).astype(jnp.int32)
    before = jnp.cumsum(onehot, axis=0) - onehot
    slot = jnp.sum(before * onehot, axis=1)
    target = flat_ids * CAP + slot
    placer = (jnp.arange(experts * CAP, dtype=jnp.int32)[:, None] == target[None, :]).astype(
        jnp.bfloat16
    )
    placer_tok = jnp.sum(
        placer.reshape(experts * CAP, tok_rows, picks).astype(jnp.float32), axis=2
    ).astype(jnp.bfloat16)
    grad32 = cotangent.astype(jnp.float32)
    scaled_grad = (
        (route_weights[:, :, None] * grad32[:, None, :])
        .astype(jnp.bfloat16)
        .reshape(tok_rows * picks, width)
    )
    send_x = (
        jnp.dot(placer_tok, tokens, preferred_element_type=jnp.float32)
        .astype(jnp.bfloat16)
        .reshape(experts, CAP, width)
    )
    send_g = (
        jnp.dot(placer, scaled_grad, preferred_element_type=jnp.float32)
        .astype(jnp.bfloat16)
        .reshape(experts, CAP, width)
    )
    gate_w = gate_weight[0]
    up_w = up_weight[0]
    down_w = down_weight[0]
    y_back, dx_back = exchange(send_x, send_g, gate_w, up_w, down_w, experts, pair, width)
    picked_y = lax.dot_general(
        placer, y_back, (((0,), (0,)), ((), ())), preferred_element_type=jnp.float32
    ).reshape(tok_rows, picks, width)
    picked_dx = lax.dot_general(
        placer, dx_back, (((0,), (0,)), ((), ())), preferred_element_type=jnp.float32
    ).reshape(tok_rows, picks, width)
    mixed = jnp.sum(route_weights[:, :, None] * picked_y, axis=1).astype(jnp.bfloat16)
    grad_tokens = jnp.sum(picked_dx, axis=1).astype(jnp.bfloat16)
    grad_weights = jnp.sum(grad32[:, None, :] * picked_y, axis=2)
    return (mixed, grad_tokens, grad_weights)


def solution(mesh):
    in_specs = (
        P(("groups", "expert", "tensor"), None),
        P(("groups", "expert", "tensor"), None),
        P(("groups", "expert", "tensor"), None),
        P(("groups", "expert", "tensor"), None),
        P("expert", None, "tensor"),
        P("expert", None, "tensor"),
        P("expert", "tensor", None),
        P(("groups", "expert", "tensor"), None),
    )
    out_specs = (
        P(("groups", "expert", "tensor"), None),
        P(("groups", "expert", "tensor"), None),
        P(("groups", "expert", "tensor"), None),
    )
    return jax.shard_map(body, mesh=mesh, in_specs=in_specs, out_specs=out_specs, check_vma=False)
```
